32 devices in a mesh: parts: 1, leaf: 32 (over z, y, x, core).
Axes of the slice: x: 2, y: 2, z: 4, core: 2. Of those that a mesh axis runs over, the one named last changes fastest.
Arguments:
- points: bfloat16 [640, 8, 256], P(('parts', 'leaf')), may hold values from -3 to 6
- charges: bfloat16 [640, 32, 256], P(('parts', 'leaf')), may hold values from -0.625 to 0.625
- basis: bfloat16 [640, 256, 128], P(('parts', 'leaf')), may hold values from -0.375 to 0.375
- transfer: bfloat16 [640, 128, 128], P(('parts', 'leaf')), may hold values from -0.5 to 0.5
- skeleton: bfloat16 [640, 8, 128], P(('parts', 'leaf')), may hold values from -3 to 6
- top_skeleton: bfloat16 [16, 8, 128], P('parts'), may hold values from -5 to 8
- near_mask: int32 [640, 14], P(('parts', 'leaf')), may hold values 0 or 1
- remote_dev: int32 [640, 12], P(('parts', 'leaf')), may hold values from 0 to 30, all different within a row; in each aligned block of 20 rows (0 to 19, 20 to 39, ...) at most 9 rows name the same one
- remote_leaf: int32 [640, 12], P(('parts', 'leaf')), may hold values from 0 to 19
- far_mask: int32 [640, 6], P(('parts', 'leaf')), may hold values 0 or 1
- top_far: int32 [16, 8], P('parts'), may hold values from 0 to 15, as said below
Outputs:
- product: float32 [640, 32, 256], P(('parts', 'leaf'))
The draws below stay inside these ranges and needn't reach their ends.
Inputs may be any that keep to these rules, and one draw needn't show every extreme that they name: `remote_dev`: each row names 12 different values; the 20 rows of one device name any value at most 9 times, a bound that some block reaches. `top_far`: each row names 8 different nodes, never its own.
All inputs are finite; a program needn't handle non-finite values. No bound on the sum of `near_mask` or of `far_mask` on one device may be relied on, other than what follows from the above.
Results may differ from the reference program's by a relative error of at most 0.0039.
Values may be sent and summed in bfloat16 or wider, within the bound.
A program may use at most 64 MiB of HBM per device.

```python
import math
import jax
import jax.numpy as jnp
import numpy as np
from jax import lax

DIM = 8
NRHS = 32
LEAF_PTS = 256
RANK = 128
R = 7
NREM = 12
FW = 3
TOPN = 16
FART = 8
LEAVES_DEV = 20
LEAVES = 640
MOST = 9
N_LEAF = 32


def leaf_centers(leaf_ids, coords):
    component = jnp.arange(coords, dtype=jnp.int32)
    low_bits = jnp.right_shift(leaf_ids[:, None], component[None, :]) & 1
    high_bits = jnp.right_shift(leaf_ids[:, None], component[None, :] + coords) & 1
    return (low_bits + 2 * high_bits).astype(jnp.float32)


def cloud(key, leaf_ids, count, spread):
    centers = leaf_centers(leaf_ids, DIM)
    noise = jnp.clip(jax.random.normal(key, (leaf_ids.shape[0], DIM, count), jnp.float32), -6.0, 6.0)
    return (centers[:, :, None] + spread * noise).astype(jnp.bfloat16)


def draw_points(key, part):
    key = jax.random.fold_in(key, 11)
    return cloud(key, jnp.arange(LEAVES, dtype=jnp.int32), LEAF_PTS, 0.5)


def draw_skeleton(key, part):
    key = jax.random.fold_in(key, 12)
    return cloud(key, jnp.arange(LEAVES, dtype=jnp.int32), RANK, 0.5)


def draw_top_skeleton(key, part):
    key = jax.random.fold_in(key, 13)
    span = LEAVES // TOPN
    leaf_ids = jnp.arange(TOPN, dtype=jnp.int32) * span + span // 2
    return cloud(key, leaf_ids, RANK, 0.7)


def draw_top_far(key, part):
    key = jax.random.fold_in(key, 14)
    scores = jax.random.randint(key, (TOPN, TOPN - 1), 0, 4096) * TOPN + jnp.arange(TOPN - 1, dtype=jnp.int32)[None, :]
    picked = lax.top_k(scores, FART)[1].astype(jnp.int32)
    return ((jnp.arange(TOPN, dtype=jnp.int32)[:, None] + 1 + picked) % TOPN).astype(jnp.int32)


def touch_ends(result, own_key, smallest, top_value):
    longest = result.shape.index(max(result.shape))
    spots = []
    for shift in (0, 1):
        where = [jax.random.randint(jax.random.fold_in(own_key, axis), (), 0, length) for axis, length in enumerate(result.shape)]
        where[longest] = (where[longest] + shift) % result.shape[longest]
        spots.append(tuple(where))
    return result.at[spots[0]].set(smallest).at[spots[1]].set(top_value)


def levels(own_key, shape, pieces, least, largest):
    def one(axis_at, parts):
        draws = jax.random.uniform(jax.random.fold_in(jax.random.fold_in(own_key, 6), axis_at), (parts,), jnp.float32, least / len(pieces), largest / len(pieces))
        return jnp.repeat(jnp.exp(draws), shape[axis_at] // parts).reshape((-1,) + (1,) * (len(shape) - axis_at - 1))

    factor_of = one(*pieces[0])
    for cut in pieces[1:]:
        factor_of = factor_of * one(*cut)
    return factor_of


def assign_block(own_key, own, number, rows, count, top, most, slope):
    order = jax.random.permutation(own_key, count)
    packed, usual = portions_of(count, rows * top, most, slope, True), portions_of(count, rows * top, most, slope, False)
    places = jnp.arange(count)

    def named(sizes, offset_by):
        used = int((sizes > 0).sum())
        fixed = max(1, used // 4)
        passed = fixed + (places - fixed + offset_by * (used - fixed)) % max(1, count - fixed)
        return jnp.zeros((count,), jnp.int32).at[order[jnp.where(places < fixed, places, passed)]].set(jnp.asarray(sizes, jnp.int32))

    sizes = jnp.where(number % 4 == 0, named(packed, number // 4), named(usual, number - number // 4 - 1))
    mixed = jax.random.permutation(jax.random.fold_in(own, 3), count)
    giver, receiver = mixed[0:count // 2 * 2:2], mixed[1:count // 2 * 2:2]
    margin = jnp.minimum(sizes[giver] - 1, most - sizes[receiver]) // 2
    margin = jnp.where((giver == order[0]) | (receiver == order[0]) | (sizes[receiver] == 0), 0, jnp.maximum(margin, 0))
    passed = jax.random.randint(jax.random.fold_in(own, 4), (count // 2,), 0, 1 << 20) % (margin + 1)
    sizes = sizes.at[giver].add(-passed).at[receiver].add(passed)
    items = jnp.searchsorted(jnp.cumsum(sizes), jnp.arange(rows * top), side="right").astype(jnp.int32)
    table = items.reshape(top, rows).T
    table = table[jax.random.permutation(jax.random.fold_in(own, 1), rows)]
    offset_by = jax.random.randint(jax.random.fold_in(own, 2), (rows, 1), 0, top)
    return jnp.take_along_axis(table, (jnp.arange(top)[None, :] + offset_by) % top, axis=1)


def portions_of(number_of, total, limit, slope, full):
    loads = [(1 << 20) // math.isqrt(grade ** slope) + 1 for grade in range(1, number_of + 1)]
    largest = limit if full else min(limit, max(-(-total // number_of), total * loads[0] // sum(loads)))
    least = 1 if total - largest >= number_of - 1 else 0
    holding, spare = [largest] + [least] * (number_of - 1), total - largest - least * (number_of - 1)
    while spare > 0:
        candidates = [i for i in range(1, number_of) if holding[i] < largest] or [i for i in range(1, number_of) if holding[i] < limit]
        mass, remaining = sum([loads[i] for i in candidates]), spare
        for i in candidates:
            addition = min(limit - holding[i], max(1, remaining * loads[i] // mass), spare)
            holding[i] = holding[i] + addition
            spare = spare - addition
    return np.array(holding)


def scatter_about(stream_key, shape, width, limit, split=(), held_as=jnp.bfloat16):
    entries = width * jax.random.normal(stream_key, shape, jnp.float32)
    if split:
        entries = entries * levels(stream_key, shape, split, -0.22, 0.18)
    return jnp.clip(entries, -limit, limit).astype(held_as)


def setup_inputs(seed: int = 0, part: int = 0) -> dict:
    arg_keys = jax.random.split(jax.random.key(seed), 12)
    part_splits = jax.random.split(jax.random.fold_in(arg_keys[11], part), 12)
    points = draw_points(jax.random.fold_in(jax.random.fold_in(arg_keys[11], part), 71), part)
    charges = scatter_about(part_splits[1], (LEAVES, NRHS, LEAF_PTS), 0.1, 0.625, ((0, 32),))
    basis = scatter_about(part_splits[2], (LEAVES, LEAF_PTS, RANK), LEAF_PTS ** -0.5, 0.375, ((0, 32),))
    transfer = scatter_about(part_splits[3], (LEAVES, RANK, RANK), RANK ** -0.5, 0.5, ((0, 32),))
    skeleton = draw_skeleton(jax.random.fold_in(jax.random.fold_in(arg_keys[11], part), 71), part)
    top_skeleton = draw_top_skeleton(jax.random.fold_in(jax.random.fold_in(arg_keys[11], part), 71), part)
    near_mask = touch_ends((jax.random.randint(part_splits[6], (LEAVES, 2 * R), 0, 4) < 3).astype(jnp.int32), jax.random.fold_in(part_splits[6], 1), 0, 1)
    remote_dev_keys = jax.random.split(jax.random.fold_in(part_splits[7], 1), LEAVES // LEAVES_DEV)
    remote_dev_turns = jax.random.permutation(jax.random.fold_in(part_splits[7], 3), LEAVES // LEAVES_DEV)
    remote_dev = jax.vmap(lambda own, number: assign_block(jax.random.fold_in(part_splits[7], 2), own, number, LEAVES_DEV, N_LEAF - 1, NREM, MOST, 2))(remote_dev_keys, remote_dev_turns).reshape((LEAVES, NREM))
    remote_leaf = touch_ends(jax.random.randint(part_splits[8], (LEAVES, NREM), 0, LEAVES_DEV), jax.random.fold_in(part_splits[8], 1), 0, LEAVES_DEV - 1).astype(jnp.int32)
    far_mask = touch_ends((jax.random.randint(part_splits[9], (LEAVES, 2 * FW), 0, 2) < 1).astype(jnp.int32), jax.random.fold_in(part_splits[9], 1), 0, 1)
    top_far = draw_top_far(jax.random.fold_in(jax.random.fold_in(arg_keys[11], part), 71), part)
    return {"points": points, "charges": charges, "basis": basis, "transfer": transfer, "skeleton": skeleton, "top_skeleton": top_skeleton, "near_mask": near_mask, "remote_dev": remote_dev, "remote_leaf": remote_leaf, "far_mask": far_mask, "top_far": top_far}


ROOT_THREE = math.sqrt(3.0)
LENGTH_SCALE = 1.0

def matern(targets, sources):
    squares = 0.0
    for component in range(targets.shape[-2]):
        offset_gap = targets[..., component, :, None] - sources[..., component, None, :]
        squares = squares + offset_gap * offset_gap
    scaled = ROOT_THREE * jnp.sqrt(squares) / LENGTH_SCALE
    return (1.0 + scaled) * jnp.exp(-scaled)

def reference(points, charges, basis, transfer, skeleton, top_skeleton, near_mask, remote_dev, remote_leaf, far_mask, top_far):
    leaf_ids = jnp.arange(LEAVES, dtype=jnp.int32)
    points_wide = points.astype(jnp.float32)
    leaf_pack = jnp.concatenate([points, charges], axis=1)
    padded = jnp.pad(leaf_pack, ((R, R), (0, 0), (0, 0)))
    owner = leaf_ids // LEAVES_DEV
    remote_src = ((owner[:, None] + 1 + remote_dev) % N_LEAF * LEAVES_DEV + remote_leaf).astype(jnp.int32)
    ones_column = jnp.ones((LEAVES, 1), jnp.bfloat16)
    ones_remote = jnp.ones((LEAVES, NREM), jnp.bfloat16)
    mask_all = jnp.concatenate([near_mask[:, :R].astype(jnp.bfloat16), ones_column, near_mask[:, R:].astype(jnp.bfloat16), ones_remote], axis=1)

    def near_one(leaf_index):
        window = lax.dynamic_slice_in_dim(padded, leaf_index, 2 * R + 1, 0)
        sources = jnp.concatenate([window, leaf_pack[remote_src[leaf_index]]], axis=0)
        kernel = matern(points_wide[leaf_index], sources[:, :DIM].astype(jnp.float32)).astype(jnp.bfloat16)
        kernel = kernel * mask_all[leaf_index][:, None, None]
        return jnp.einsum('snq,spq->np', sources[:, DIM:].astype(jnp.float32), kernel.astype(jnp.float32))
    near_field = lax.map(near_one, leaf_ids)
    weights = jnp.einsum('lnp,lpr->lnr', charges.astype(jnp.float32), basis.astype(jnp.float32)).astype(jnp.bfloat16)
    far_pack = jnp.concatenate([skeleton, weights], axis=1)
    far_padded = jnp.pad(far_pack, ((R + FW, R + FW), (0, 0), (0, 0)))
    far_flags = far_mask.astype(jnp.bfloat16)

    def far_one(leaf_index):
        below = lax.dynamic_slice_in_dim(far_padded, leaf_index, FW, 0)
        above = lax.dynamic_slice_in_dim(far_padded, leaf_index + 2 * R + FW + 1, FW, 0)
        sources = jnp.concatenate([below, above], axis=0)
        kernel = matern(skeleton[leaf_index].astype(jnp.float32), sources[:, :DIM].astype(jnp.float32)).astype(jnp.bfloat16)
        kernel = kernel * far_flags[leaf_index][:, None, None]
        return jnp.einsum('snq,spq->np', sources[:, DIM:].astype(jnp.float32), kernel.astype(jnp.float32))
    far_terms = lax.map(far_one, leaf_ids)
    lifted = jnp.einsum('lrs,lnr->lns', transfer.astype(jnp.float32), weights.astype(jnp.float32))
    node_weights = lax.optimization_barrier(jnp.sum(lifted.reshape(TOPN, LEAVES // TOPN, NRHS, RANK), axis=1))
    node_ids = jnp.arange(TOPN, dtype=jnp.int32)

    def node_one(node_index):
        far_nodes = top_far[node_index]
        node_kernel = matern(top_skeleton[node_index].astype(jnp.float32), top_skeleton[far_nodes].astype(jnp.float32))
        return jnp.einsum('mrs,mns->nr', node_kernel, node_weights[far_nodes], precision=lax.Precision.HIGHEST)
    expansion = lax.map(node_one, node_ids).astype(jnp.bfloat16)
    node_of_leaf = leaf_ids // (LEAVES // TOPN)
    down = jnp.einsum('lrs,lns->lnr', transfer.astype(jnp.float32), expansion[node_of_leaf].astype(jnp.float32))
    local_terms = (far_terms + down).astype(jnp.bfloat16)
    far_field = jnp.einsum('lpr,lnr->lnp', basis.astype(jnp.float32), local_terms.astype(jnp.float32))
    return near_field + far_field
```

```python
import functools
import math

import jax
import jax.numpy as jnp
from jax import lax
from jax.experimental import pallas as pl
from jax.experimental.pallas import tpu as pltpu
from jax.sharding import PartitionSpec as P

ROOT_THREE = math.sqrt(3.0)
LENGTH_SCALE = 1.0
ALPHA = 3.0 / (LENGTH_SCALE * LENGTH_SCALE)
UNROLL = 8
VMEM_LIMIT = 56 * 2**20


def with_halo(array, sides, width):
    for axis, dim in sides:
        count, length = (lax.axis_size(axis), array.shape[dim])
        up = [(i, (i + 1) % count) for i in range(count - 1)]
        down = [(j, i) for i, j in up]
        last = lax.slice_in_dim(array, length - width, length, axis=dim)
        initial = lax.slice_in_dim(array, 0, width, axis=dim)
        before = lax.ppermute(last, axis, up)
        after = lax.ppermute(initial, axis, down)
        array = jnp.concatenate([before, array, after], axis=dim)
    return array


def matern(targets, sources):
    squares = 0.0
    for component in range(targets.shape[-2]):
        offset_gap = targets[..., component, :, None] - sources[..., component, None, :]
        squares = squares + offset_gap * offset_gap
    scaled = ROOT_THREE * jnp.sqrt(squares) / LENGTH_SCALE
    return (1.0 + scaled) * jnp.exp(-scaled)


def reduced(value):
    return lax.reduce_precision(value, 8, 7)


def rounded(value):
    return value.astype(jnp.bfloat16).astype(jnp.float32)


def three_parts(value, narrow):
    high = narrow(value)
    middle = narrow(value - high)
    return high, middle, narrow(value - high - middle)


def target_side(points):
    wide = points.astype(jnp.float32)
    cross = three_parts(-2.0 * ALPHA * wide, reduced)
    norms = three_parts(ALPHA * jnp.sum(wide * wide, axis=1, keepdims=True), reduced)
    one = jnp.ones_like(norms[0])
    zero = jnp.zeros_like(one)
    rows = jnp.concatenate([*cross, *norms, one, one, one, zero, zero], axis=1)
    return jnp.swapaxes(rows.astype(jnp.bfloat16), 1, 2)


def source_side(points):
    high, middle, low = three_parts(
        ALPHA * jnp.sum(points * points, axis=0, keepdims=True), rounded
    )
    row = lax.broadcasted_iota(jnp.int32, points.shape, 0)
    tail = jnp.where(
        row < 3,
        1.0,
        jnp.where(row == 3, high, jnp.where(row == 4, middle, jnp.where(row == 5, low, 0.0))),
    )
    return jnp.concatenate([points, points, points, tail], axis=0).astype(jnp.bfloat16)


def kernel_values(squares):
    squares = jnp.maximum(squares, 1e-20)
    scaled = squares * lax.rsqrt(squares)
    return ((1.0 + scaled) * jnp.exp(-scaled)).astype(jnp.bfloat16)


def dot_last(a, b):
    return lax.dot_general(a, b, (((1,), (1,)), ((), ())), preferred_element_type=jnp.float32)


def pair_kernel(rhs, has_base, count_ref, source_ref, target_ref, scale_ref, side_ref, pack_ref, *rest):
    out_ref = rest[-1]
    out_ref[...] = rest[0][...] if has_base else jnp.zeros_like(out_ref)

    def step(number, carry):
        pairs = []
        for slot in range(UNROLL):
            entry = number * UNROLL + slot
            block = pack_ref[source_ref[entry]]
            squares = jnp.dot(
                side_ref[target_ref[entry]],
                source_side(block[rhs:].astype(jnp.float32)),
                preferred_element_type=jnp.float32,
            )
            pairs.append((entry, block, squares))
        sums = []
        for entry, block, squares in pairs:
            charges = block[:rhs] * scale_ref[entry].astype(jnp.bfloat16)
            sums.append((target_ref[entry], dot_last(charges, kernel_values(squares))))
        for target, term in sums:
            out_ref[target] += term
        return carry

    lax.fori_loop(0, (count_ref[0] + UNROLL - 1) // UNROLL, step, 0)


def sum_pairs(pairs, side, pack, base=None, name="pairs"):
    leaves, length = side.shape[:2]
    rhs = pack.shape[1] - 8
    scalars = pl.BlockSpec(memory_space=pltpu.SMEM)
    vectors = pl.BlockSpec(memory_space=pltpu.VMEM)
    extra = [] if base is None else [base]
    work = pairs[1].shape[0] * length * pack.shape[2]
    return pl.pallas_call(
        functools.partial(pair_kernel, rhs, base is not None),
        out_shape=jax.ShapeDtypeStruct((leaves, rhs, length), jnp.float32),
        in_specs=[scalars] * 4 + [vectors] * (2 + len(extra)),
        out_specs=vectors,
        compiler_params=pltpu.CompilerParams(vmem_limit_bytes=VMEM_LIMIT),
        cost_estimate=pl.CostEstimate(
            flops=2 * work * 64, bytes_accessed=2 * pack.size, transcendentals=2 * work
        ),
        name=name,
    )(*pairs, side, pack, *extra)


def far_kernel(rhs, near, far, mask_ref, side_ref, pack_ref, transfer_ref, expansion_ref, basis_ref, base_ref, out_ref):
    def one(leaf, carry):
        local = dot_last(expansion_ref[...], transfer_ref[leaf])
        for slot in range(2 * far):
            offset = slot if slot < far else slot + 2 * near + 1
            block = pack_ref[leaf + offset]
            squares = jnp.dot(
                side_ref[leaf],
                source_side(block[rhs:].astype(jnp.float32)),
                preferred_element_type=jnp.float32,
            )
            flag = mask_ref[leaf, slot].astype(jnp.float32).astype(jnp.bfloat16)
            local = local + dot_last(block[:rhs] * flag, kernel_values(squares))
        out_ref[leaf] = base_ref[leaf] + dot_last(local.astype(jnp.bfloat16), basis_ref[leaf])
        return carry

    lax.fori_loop(0, out_ref.shape[0], one, 0)


def listed(keep, source, target):
    keep, source, target = keep.reshape(-1), source.reshape(-1), target.reshape(-1)
    total = keep.shape[0]
    room = -(-total // UNROLL) * UNROLL
    ids = jnp.arange(total, dtype=jnp.int32)
    place = jnp.sum(jnp.where((ids[None, :] < ids[:, None]) & keep[None, :], 1, 0), axis=1)
    slots = jnp.arange(room, dtype=jnp.int32)
    hit = (place[None, :] == slots[:, None]) & keep[None, :]
    sources = jnp.sum(jnp.where(hit, source[None, :], 0), axis=1)
    targets = jnp.sum(jnp.where(hit, target[None, :], 0), axis=1)
    count = jnp.sum(keep.astype(jnp.int32))
    scales = (slots < count).astype(jnp.float32)
    return count.reshape(1), sources.astype(jnp.int32), targets.astype(jnp.int32), scales


def per_device(
    points,
    charges,
    basis,
    transfer,
    skeleton,
    top_skeleton,
    near_mask,
    remote_dev,
    remote_leaf,
    far_mask,
    top_far,
):
    devices = lax.axis_size("leaf")
    device = lax.axis_index("leaf")
    local_count, rhs = charges.shape[:2]
    near_reach = near_mask.shape[1] // 2
    far_reach = far_mask.shape[1] // 2
    node_count = top_skeleton.shape[0]
    leaf_pack = jnp.concatenate([charges, points], axis=1)
    gathered = lax.all_gather(leaf_pack, "leaf", axis=0, tiled=True)

    weights = jnp.einsum("lnp,lpr->lnr", charges, basis, preferred_element_type=jnp.float32).astype(
        jnp.bfloat16
    )
    far_pack = jnp.concatenate([weights, skeleton], axis=1)
    far_wide = with_halo(far_pack, (("leaf", 0),), near_reach + far_reach)
    partial_weights = jnp.einsum(
        "lrs,lnr->ns", transfer, weights, preferred_element_type=jnp.float32
    )
    per_node = devices // node_count
    own_node = device // per_node
    node_weights = lax.all_gather(partial_weights, "leaf", axis=0)
    node_weights = node_weights.reshape((node_count, per_node) + partial_weights.shape).sum(axis=1)
    far_nodes = top_far[own_node]
    node_kernel = matern(
        top_skeleton[own_node].astype(jnp.float32), top_skeleton[far_nodes].astype(jnp.float32)
    )
    expansion = jnp.einsum(
        "mrs,mns->nr", node_kernel, node_weights[far_nodes], precision=lax.Precision.HIGHEST
    ).astype(jnp.bfloat16)

    leaf_ids = jnp.arange(local_count, dtype=jnp.int32)
    reach = jnp.arange(-near_reach, near_reach + 1, dtype=jnp.int32)
    window = leaf_ids[:, None] + reach[None, :]
    inside = (window >= 0) & (window < local_count)
    wanted = jnp.concatenate(
        [near_mask[:, :near_reach], jnp.ones((local_count, 1), jnp.int32), near_mask[:, near_reach:]],
        axis=1,
    ) != 0
    window_targets = jnp.broadcast_to(leaf_ids[:, None], window.shape)
    own_pairs = listed(wanted & inside, window, window_targets)
    distant = window + device * local_count
    crossing = wanted & ~inside & (distant >= 0) & (distant < devices * local_count)
    remote = (device + 1 + remote_dev) % devices * local_count + remote_leaf
    other_pairs = listed(
        jnp.concatenate([crossing, jnp.ones(remote.shape, bool)], axis=1),
        jnp.concatenate([distant, remote], axis=1),
        jnp.broadcast_to(leaf_ids[:, None], (local_count, window.shape[1] + remote.shape[1])),
    )

    side = target_side(points)
    own_field = sum_pairs(own_pairs, side, leaf_pack, name="own_pairs")
    scalars = pl.BlockSpec(memory_space=pltpu.SMEM)
    vectors = pl.BlockSpec(memory_space=pltpu.VMEM)
    with_far = pl.pallas_call(
        functools.partial(far_kernel, rhs, near_reach, far_reach),
        out_shape=jax.ShapeDtypeStruct(own_field.shape, jnp.float32),
        in_specs=[scalars] + [vectors] * 6,
        out_specs=vectors,
        compiler_params=pltpu.CompilerParams(vmem_limit_bytes=VMEM_LIMIT),
        name="far_field",
    )(far_mask, target_side(skeleton), far_wide, transfer, expansion, basis, own_field)
    return sum_pairs(other_pairs, side, gathered, with_far, name="other_pairs")


def solution(mesh):
    placed = (
        P(("parts", "leaf"), None, None),
        P(("parts", "leaf"), None, None),
        P(("parts", "leaf"), None, None),
        P(("parts", "leaf"), None, None),
        P(("parts", "leaf"), None, None),
        P("parts", None, None),
        P(("parts", "leaf"), None),
        P(("parts", "leaf"), None),
        P(("parts", "leaf"), None),
        P(("parts", "leaf"), None),
        P("parts", None),
    )
    return jax.shard_map(
        per_device,
        mesh=mesh,
        in_specs=placed,
        out_specs=P(("parts", "leaf"), None, None),
        check_vma=False,
    )
```

```python
import functools
import math

import jax
import jax.numpy as jnp
from jax import lax
from jax.experimental import pallas as pl
from jax.experimental.pallas import tpu as pltpu
from jax.sharding import PartitionSpec as P

ROOT_THREE = math.sqrt(3.0)
LENGTH_SCALE = 1.0
ALPHA = 3.0 / (LENGTH_SCALE * LENGTH_SCALE)
UNROLL = 8
VMEM_LIMIT = 56 * 2**20


def with_halo(array, sides, width):
    for axis, dim in sides:
        count, length = (lax.axis_size(axis), array.shape[dim])
        up = [(i, (i + 1) % count) for i in range(count - 1)]
        down = [(j, i) for i, j in up]
        last = lax.slice_in_dim(array, length - width, length, axis=dim)
        initial = lax.slice_in_dim(array, 0, width, axis=dim)
        before = lax.ppermute(last, axis, up)
        after = lax.ppermute(initial, axis, down)
        array = jnp.concatenate([before, array, after], axis=dim)
    return array


def matern(targets, sources):
    squares = 0.0
    for component in range(targets.shape[-2]):
        offset_gap = targets[..., component, :, None] - sources[..., component, None, :]
        squares = squares + offset_gap * offset_gap
    scaled = ROOT_THREE * jnp.sqrt(squares) / LENGTH_SCALE
    return (1.0 + scaled) * jnp.exp(-scaled)


def rounded(value):
    return value.astype(jnp.bfloat16).astype(jnp.float32)


def three_parts(value, narrow):
    high = narrow(value)
    middle = narrow(value - high)
    return high, middle, narrow(value - high - middle)


def target_side(points):
    cross = three_parts(-2.0 * ALPHA * points, rounded)
    high, middle, low = three_parts(
        ALPHA * jnp.sum(points * points, axis=0, keepdims=True), rounded
    )
    row = lax.broadcasted_iota(jnp.int32, points.shape, 0)
    tail = jnp.where(
        row == 0,
        high,
        jnp.where(row == 1, middle, jnp.where(row == 2, low, jnp.where(row < 6, 1.0, 0.0))),
    )
    return jnp.concatenate([*cross, tail], axis=0).T.astype(jnp.bfloat16)


def sides_kernel(points_ref, skeleton_ref, points_side_ref, skeleton_side_ref):
    def one(leaf, carry):
        points_side_ref[leaf] = target_side(points_ref[leaf].astype(jnp.float32))
        skeleton_side_ref[leaf] = target_side(skeleton_ref[leaf].astype(jnp.float32))
        return carry

    lax.fori_loop(0, points_ref.shape[0], one, 0)


def target_sides(*clouds):
    vectors = pl.BlockSpec(memory_space=pltpu.VMEM)
    return pl.pallas_call(
        sides_kernel,
        out_shape=[
            jax.ShapeDtypeStruct((c.shape[0], c.shape[2], 4 * c.shape[1]), jnp.bfloat16)
            for c in clouds
        ],
        in_specs=[vectors] * 2,
        out_specs=[vectors] * 2,
        compiler_params=pltpu.CompilerParams(vmem_limit_bytes=VMEM_LIMIT),
        name="target_sides",
    )(*clouds)


def source_side(points):
    high, middle, low = three_parts(
        ALPHA * jnp.sum(points * points, axis=0, keepdims=True), rounded
    )
    row = lax.broadcasted_iota(jnp.int32, points.shape, 0)
    tail = jnp.where(
        row < 3,
        1.0,
        jnp.where(row == 3, high, jnp.where(row == 4, middle, jnp.where(row == 5, low, 0.0))),
    )
    return jnp.concatenate([points, points, points, tail], axis=0).astype(jnp.bfloat16)


def kernel_values(squares):
    squares = jnp.maximum(squares, 1e-20)
    scaled = squares * lax.rsqrt(squares)
    return ((1.0 + scaled) * jnp.exp(-scaled)).astype(jnp.bfloat16)


def dot_last(a, b):
    return lax.dot_general(a, b, (((1,), (1,)), ((), ())), preferred_element_type=jnp.float32)


def pair_kernel(rhs, has_base, count_ref, source_ref, target_ref, scale_ref, side_ref, pack_ref, *rest):
    out_ref = rest[-1]
    out_ref[...] = rest[0][...] if has_base else jnp.zeros_like(out_ref)

    def step(number, carry):
        pairs = []
        for slot in range(UNROLL):
            entry = number * UNROLL + slot
            block = pack_ref[source_ref[entry]]
            squares = jnp.dot(
                side_ref[target_ref[entry]],
                source_side(block[rhs:].astype(jnp.float32)),
                preferred_element_type=jnp.float32,
            )
            pairs.append((entry, block, squares))
        sums = []
        for entry, block, squares in pairs:
            charges = block[:rhs] * scale_ref[entry].astype(jnp.bfloat16)
            sums.append((target_ref[entry], dot_last(charges, kernel_values(squares))))
        for target, term in sums:
            out_ref[target] += term
        return carry

    lax.fori_loop(0, (count_ref[0] + UNROLL - 1) // UNROLL, step, 0)


def sum_pairs(pairs, side, pack, base=None, name="pairs"):
    leaves, length = side.shape[:2]
    rhs = pack.shape[1] - 8
    scalars = pl.BlockSpec(memory_space=pltpu.SMEM)
    vectors = pl.BlockSpec(memory_space=pltpu.VMEM)
    extra = [] if base is None else [base]
    return pl.pallas_call(
        functools.partial(pair_kernel, rhs, base is not None),
        out_shape=jax.ShapeDtypeStruct((leaves, rhs, length), jnp.float32),
        in_specs=[scalars] * 4 + [vectors] * (2 + len(extra)),
        out_specs=vectors,
        compiler_params=pltpu.CompilerParams(vmem_limit_bytes=VMEM_LIMIT),
        cost_estimate=pl.CostEstimate(flops=1024, bytes_accessed=1024, transcendentals=0),
        name=name,
    )(*pairs, side, pack, *extra)


def far_kernel(rhs, near, far, mask_ref, side_ref, pack_ref, transfer_ref, expansion_ref, basis_ref, base_ref, out_ref):
    def one(leaf, carry):
        local = dot_last(expansion_ref[...], transfer_ref[leaf])
        for slot in range(2 * far):
            offset = slot if slot < far else slot + 2 * near + 1
            block = pack_ref[leaf + offset]
            squares = jnp.dot(
                side_ref[leaf],
                source_side(block[rhs:].astype(jnp.float32)),
                preferred_element_type=jnp.float32,
            )
            flag = mask_ref[leaf, slot].astype(jnp.float32).astype(jnp.bfloat16)
            local = local + dot_last(block[:rhs] * flag, kernel_values(squares))
        out_ref[leaf] = base_ref[leaf] + dot_last(local.astype(jnp.bfloat16), basis_ref[leaf])
        return carry

    lax.fori_loop(0, out_ref.shape[0], one, 0)


def listed(keep, source, target):
    keep, source, target = keep.reshape(-1), source.reshape(-1), target.reshape(-1)
    total = keep.shape[0]
    room = -(-total // UNROLL) * UNROLL
    ids = jnp.arange(total, dtype=jnp.int32)
    place = jnp.sum(jnp.where((ids[None, :] < ids[:, None]) & keep[None, :], 1, 0), axis=1)
    slots = jnp.arange(room, dtype=jnp.int32)
    hit = (place[None, :] == slots[:, None]) & keep[None, :]
    sources = jnp.sum(jnp.where(hit, source[None, :], 0), axis=1)
    targets = jnp.sum(jnp.where(hit, target[None, :], 0), axis=1)
    count = jnp.sum(keep.astype(jnp.int32))
    scales = (slots < count).astype(jnp.float32)
    return count.reshape(1), sources.astype(jnp.int32), targets.astype(jnp.int32), scales


def per_device(
    points,
    charges,
    basis,
    transfer,
    skeleton,
    top_skeleton,
    near_mask,
    remote_dev,
    remote_leaf,
    far_mask,
    top_far,
):
    devices = lax.axis_size("leaf")
    device = lax.axis_index("leaf")
    local_count, rhs = charges.shape[:2]
    near_reach = near_mask.shape[1] // 2
    far_reach = far_mask.shape[1] // 2
    node_count = top_skeleton.shape[0]
    leaf_pack = jnp.concatenate([charges, points], axis=1)
    gathered = lax.all_gather(leaf_pack, "leaf", axis=0, tiled=True)

    weights = jnp.einsum("lnp,lpr->lnr", charges, basis, preferred_element_type=jnp.float32).astype(
        jnp.bfloat16
    )
    far_pack = jnp.concatenate([weights, skeleton], axis=1)
    far_wide = with_halo(far_pack, (("leaf", 0),), near_reach + far_reach)
    partial_weights = jnp.einsum(
        "lrs,lnr->ns", transfer, weights, preferred_element_type=jnp.float32
    )
    leaf_ids = jnp.arange(local_count, dtype=jnp.int32)
    reach = jnp.arange(-near_reach, near_reach + 1, dtype=jnp.int32)
    window = leaf_ids[:, None] + reach[None, :]
    inside = (window >= 0) & (window < local_count)
    wanted = jnp.concatenate(
        [near_mask[:, :near_reach], jnp.ones((local_count, 1), jnp.int32), near_mask[:, near_reach:]],
        axis=1,
    ) != 0
    window_targets = jnp.broadcast_to(leaf_ids[:, None], window.shape)
    own_pairs = listed(wanted & inside, window, window_targets)
    distant = window + device * local_count
    crossing = wanted & ~inside & (distant >= 0) & (distant < devices * local_count)
    remote = (device + 1 + remote_dev) % devices * local_count + remote_leaf
    other_pairs = listed(
        jnp.concatenate([crossing, jnp.ones(remote.shape, bool)], axis=1),
        jnp.concatenate([distant, remote], axis=1),
        jnp.broadcast_to(leaf_ids[:, None], (local_count, window.shape[1] + remote.shape[1])),
    )

    side, far_side = target_sides(points, skeleton)
    own_field = sum_pairs(own_pairs, side, leaf_pack, name="own_pairs")
    partial_weights, own_field = lax.optimization_barrier((partial_weights, own_field))
    per_node = devices // node_count
    own_node = device // per_node
    node_weights = lax.all_gather(partial_weights, "leaf", axis=0)
    node_weights = node_weights.reshape((node_count, per_node) + partial_weights.shape).sum(axis=1)
    far_nodes = top_far[own_node]
    node_kernel = matern(
        top_skeleton[own_node].astype(jnp.float32), top_skeleton[far_nodes].astype(jnp.float32)
    )
    expansion = jnp.einsum(
        "mrs,mns->nr", node_kernel, node_weights[far_nodes], precision=lax.Precision.HIGHEST
    ).astype(jnp.bfloat16)

    scalars = pl.BlockSpec(memory_space=pltpu.SMEM)
    vectors = pl.BlockSpec(memory_space=pltpu.VMEM)
    with_far = pl.pallas_call(
        functools.partial(far_kernel, rhs, near_reach, far_reach),
        out_shape=jax.ShapeDtypeStruct(own_field.shape, jnp.float32),
        in_specs=[scalars] + [vectors] * 6,
        out_specs=vectors,
        compiler_params=pltpu.CompilerParams(vmem_limit_bytes=VMEM_LIMIT),
        name="far_field",
    )(far_mask, far_side, far_wide, transfer, expansion, basis, own_field)
    return sum_pairs(other_pairs, side, gathered, with_far, name="other_pairs")


def solution(mesh):
    placed = (
        P(("parts", "leaf"), None, None),
        P(("parts", "leaf"), None, None),
        P(("parts", "leaf"), None, None),
        P(("parts", "leaf"), None, None),
        P(("parts", "leaf"), None, None),
        P("parts", None, None),
        P(("parts", "leaf"), None),
        P(("parts", "leaf"), None),
        P(("parts", "leaf"), None),
        P(("parts", "leaf"), None),
        P("parts", None),
    )
    return jax.shard_map(
        per_device,
        mesh=mesh,
        in_specs=placed,
        out_specs=P(("parts", "leaf"), None, None),
        check_vma=False,
    )
```
